32 devices in a mesh: groups: 2 (over x), tp: 16 (over z, y, core).
Axes of the slice: x: 2, y: 2, z: 4, core: 2. Of those that a mesh axis runs over, the one named last changes fastest.
Arguments:
- hidden: bfloat16 [256, 28672], P('groups', 'tp'), parts along dimension 0, may hold values from -6 to 6
- down_weight: bfloat16 [28672, 8192], P('tp'), may hold values from -0.046875 to 0.046875
- adapter_down_weight: bfloat16 [16, 64, 28672], P('tp'), may hold values from -0.03125 to 0.03125
- adapter_up_weight: bfloat16 [16, 64, 8192], P('tp'), may hold values from -0.75 to 0.75
- row_adapter_ids: int32 [256], P('groups'), parts along dimension 0, may hold values from 0 to 15, as said below
- adapter_holder: int32 [16], replicated, may hold values from 0 to 15, each once
Outputs:
- mixed: bfloat16 [256, 8192], P('groups', 'tp'), parts along dimension 0
The draws below stay inside these ranges and needn't reach their ends.
There are 2 independent parts, one for each index of `groups`. The reference program is written for one: setup_inputs(seed, part) draws one part's arguments, and reference() takes and returns one part's arrays. A program takes and returns all parts, laid end to end along the dimension named above; an argument that names none is the same for every part. Nothing has to cross between parts.
Inputs may be any that keep to these rules, and one draw needn't show every extreme that they name: `row_adapter_ids`: exactly 24 rows name one adapter, and no adapter is named by more than 24 rows.
All inputs are finite; a program needn't handle non-finite values.
Results may differ from the reference program's by a relative error of at most 0.0039.
Values may be sent and summed in bfloat16 or wider, within the bound.
A program may use at most 128 MiB of HBM per device.

```python
import jax
import jax.numpy as jnp
from jax import lax

MODEL_WIDTH = 8192
HIDDEN_WIDTH = 28672
ADAPTER_RANK = 64
ROWS = 128
ADAPTER_COUNT = 16
CAP = 24


def draw_row_adapter_ids(key, part):
    key = jax.random.fold_in(key, 11)
    first, second, third = jax.random.split(key, 3)
    position = jax.random.permutation(first, ROWS).astype(jnp.int32)
    hot = jax.random.randint(second, (), 0, ADAPTER_COUNT).astype(jnp.int32)
    offset = jax.random.randint(third, (ROWS,), 0, 2).astype(jnp.int32)
    spread = (position - CAP + offset) % (ADAPTER_COUNT - 1)
    cold = spread + (spread >= hot).astype(jnp.int32)
    return jnp.where(position < CAP, hot, cold).astype(jnp.int32)


def raised(result, key, source, target, parts, factor):
    owner, partner = [(jnp.arange(result.shape[dim]) // (result.shape[dim] // parts)).reshape([-1 if axis == dim else 1 for axis in range(result.ndim)]) for dim in (source, target)]
    chosen = jax.random.permutation(key, parts)[partner]
    strong = (owner == chosen) | (owner == (partner + parts // 2) % parts)
    return jnp.where(strong, factor * result, result)


def levels(stream_key, shape, pieces, low, largest):
    loudness = 1.0
    for dim, parts in pieces:
        draws = jax.random.uniform(jax.random.fold_in(jax.random.fold_in(stream_key, 6), dim), (parts,), jnp.float32, low / len(pieces), largest / len(pieces))
        loudness = loudness * jnp.repeat(jnp.exp(draws), shape[dim] // parts).reshape((-1,) + (1,) * (len(shape) - 1 - dim))
    return loudness


def gaussian(rng, extent, width, limit, cuts=(), dtype=jnp.bfloat16):
    gain = levels(rng, extent, cuts, -0.22, 0.18) if cuts else 1.0
    values = jax.random.normal(rng, extent, jnp.float32) * width * gain
    return jnp.minimum(jnp.maximum(values, -limit), limit).astype(dtype)


def bell_draw_with(rng, extent, scale, bound, cuts, heavy, kind=jnp.bfloat16):
    entries = scale * jax.random.normal(rng, extent, jnp.float32)
    if cuts:
        entries = entries * levels(rng, extent, cuts, -0.22, 0.18)
    return jnp.clip(raised(entries, jax.random.fold_in(rng, 3), *heavy), -bound, bound).astype(kind)


def setup_inputs(seed: int = 0, part: int = 0) -> dict:
    arg_keys = jax.random.split(jax.random.key(seed), 7)
    part_keys = jax.random.split(jax.random.fold_in(arg_keys[6], part), 7)
    hidden = gaussian(part_keys[0], (ROWS, HIDDEN_WIDTH), 1.0, 6.0, ((1, 16),))
    down_weight = bell_draw_with(arg_keys[1], (HIDDEN_WIDTH, MODEL_WIDTH), HIDDEN_WIDTH ** -0.5, 0.046875, ((0, 16),), (0, 1, 16, 2.0))
    adapter_down_weight = gaussian(arg_keys[2], (ADAPTER_COUNT, ADAPTER_RANK, HIDDEN_WIDTH), HIDDEN_WIDTH ** -0.5, 0.03125, ((0, 16),))
    adapter_up_weight = gaussian(arg_keys[3], (ADAPTER_COUNT, ADAPTER_RANK, MODEL_WIDTH), ADAPTER_RANK ** -0.5, 0.75, ((0, 16),))
    row_adapter_ids = draw_row_adapter_ids(jax.random.fold_in(jax.random.fold_in(arg_keys[6], part), 71), part)
    adapter_holder = jax.random.permutation(arg_keys[5], ADAPTER_COUNT).astype(jnp.int32)
    return {"hidden": hidden, "down_weight": down_weight, "adapter_down_weight": adapter_down_weight, "adapter_up_weight": adapter_up_weight, "row_adapter_ids": row_adapter_ids, "adapter_holder": adapter_holder}


def reference(hidden, down_weight, adapter_down_weight, adapter_up_weight, row_adapter_ids, adapter_holder):
    base_output = jnp.dot(hidden, down_weight, preferred_element_type=jnp.float32)
    holder_device = adapter_holder[row_adapter_ids].astype(jnp.int32)

    def single_row(item):
        row, row_index = item
        down_factor = lax.dynamic_index_in_dim(adapter_down_weight, row_index, 0, keepdims=False)
        up_factor = lax.dynamic_index_in_dim(adapter_up_weight, row_index, 0, keepdims=False)
        reduced_state = jnp.dot(down_factor, row, preferred_element_type=jnp.float32).astype(jnp.bfloat16)
        return jnp.dot(reduced_state, up_factor, preferred_element_type=jnp.float32)

    adapter_delta = lax.map(single_row, (hidden, holder_device))
    return (base_output + adapter_delta).astype(jnp.bfloat16)
```

```python
import functools

import jax
import jax.numpy as jnp
from jax import lax
from jax.experimental import pallas as pl
from jax.experimental.pallas import tpu as pltpu
from jax.sharding import PartitionSpec as P

CAP = 24
F32 = jnp.float32
BF16 = jnp.bfloat16
LEVEL = 4


def mm(a, b):
    return jnp.dot(a, b, preferred_element_type=F32)


def kernel(
    levels, hid, ids, holder, down_hbm, a_hbm, u_hbm, out,
    w, a, u, sel, pack, got, core_out, core_in, y_out, y_in, total,
    lora_out, lora_in, z_out, z_in,
    w_sem, a_sem, u_sem, pack_s, pack_r, core_s, core_r, y_s, y_r, lora_s, lora_r, z_s, z_r,
):
    parts = levels * LEVEL
    rows, depth = hid.shape
    half = depth // 2
    width = out.shape[1]
    me = lax.axis_index("tp")
    z, y, c = me // 4, (me // 2) % 2, me % 2

    def device(dz, dy, dc):
        return ((z + dz) % levels) * 4 + ((y + dy) % 2) * 2 + (c + dc) % 2

    def back(dz, dy, dc):
        return ((z + levels - dz) % levels) * 4 + ((y + dy) % 2) * 2 + (c + dc) % 2

    def feature(zz, dy, dc):
        block = zz * 4 + ((y + dy) % 2) * 2 + (c + dc) % 2
        return pl.ds(pl.multiple_of(block * width, 128), width)

    def send(src, dst, s, r, dev):
        return pltpu.make_async_remote_copy(
            src_ref=src, dst_ref=dst, send_sem=s, recv_sem=r,
            device_id={"tp": dev}, device_id_type=pl.DeviceIdType.MESH,
        )

    phases = [(1, 1), (1, 0), (0, 1), (0, 0)]

    def w_copy(p, zz):
        dy, dc = phases[p]
        return pltpu.make_async_copy(
            down_hbm.at[:, feature(zz, dy, dc)], w.at[p * levels + zz], w_sem.at[p * levels + zz]
        )

    barrier = pltpu.get_barrier_semaphore()
    offsets = [(k // 4, (k // 2) % 2, k % 2) for k in range(parts)]
    for k in range(1, parts):
        pl.semaphore_signal(
            barrier, inc=1, device_id={"tp": device(*offsets[k])},
            device_id_type=pl.DeviceIdType.MESH,
        )
    for p in range(4):
        for zz in range(levels):
            w_copy(p, zz).start()
    a_copy = pltpu.make_async_copy(a_hbm, a, a_sem)
    u_copy = pltpu.make_async_copy(u_hbm, u, u_sem)
    a_copy.start()
    u_copy.start()

    held = (holder[...] == lax.broadcasted_iota(jnp.int32, (parts, parts), 0)).astype(F32)
    named = (ids[...] == lax.broadcasted_iota(jnp.int32, (parts, rows), 0)).astype(F32)
    owned = mm(held.astype(BF16), named.astype(BF16))
    upto = (
        lax.broadcasted_iota(jnp.int32, (rows, rows), 0)
        <= lax.broadcasted_iota(jnp.int32, (rows, rows), 1)
    ).astype(F32)
    count = mm(owned.astype(BF16), upto.astype(BF16))
    slot = jnp.where(owned > 0.5, count - 1.0, -1.0).astype(jnp.int32)
    for o in range(parts):
        sel[o] = (
            slot[o : o + 1, :] == lax.broadcasted_iota(jnp.int32, (CAP, rows), 0)
        ).astype(F32)

    def pack_level(i, carry):
        s = sel[pl.ds(i * 4, 4)].reshape(4 * CAP, rows).astype(BF16)
        t = mm(s, hid[...])
        for j in range(4):
            r = t[j * CAP : (j + 1) * CAP]
            pack[i * 4 + j] = jnp.concatenate([r[:, :half], r[:, half:]], axis=0).astype(BF16)
        return carry

    lax.fori_loop(0, levels, pack_level, 0)
    pl.semaphore_wait(barrier, parts - 1)

    pack_copies = [None] * parts
    for k in list(range(parts - 1, 0, -1)):
        dev = device(*offsets[k])
        pack_copies[k] = send(pack.at[dev], got.at[k], pack_s.at[k], pack_r.at[k], dev)
        pack_copies[k].start()

    def core_copy(i):
        return send(core_out.at[i], core_in.at[i], core_s.at[i], core_r.at[i], device(0, 0, 1))

    def y_copy(i):
        return send(y_out.at[i], y_in.at[i], y_s.at[i], y_r.at[i], device(0, 1, 0))

    def product(p, zz):
        w_copy(p, zz).wait()
        return mm(hid[...], w[p * levels + zz])

    def to_core(base, p):
        def body(zz, carry):
            core_out[base + zz] = product(p, zz)
            core_copy(base + zz).start()
            return carry
        lax.fori_loop(0, levels, body, 0)

    def to_y(zz, carry):
        t = product(1, zz)
        core_copy(zz).wait_recv()
        y_out[zz] = (t + core_in[zz]).astype(BF16)
        y_copy(zz).start()
        return carry

    def keep(zz, carry):
        t = product(3, zz)
        core_copy(levels + zz).wait_recv()
        t = t + core_in[levels + zz]
        y_copy(zz).wait_recv()
        total[zz] = t + y_in[zz].astype(F32)
        return carry

    to_core(0, 0)
    lax.fori_loop(0, levels, to_y, 0)
    to_core(levels, 2)
    lax.fori_loop(0, levels, keep, 0)

    a_copy.wait()
    low = jnp.zeros((CAP, a.shape[0]), F32)
    for k in range(parts):
        src = back(*offsets[k])
        if k == 0:
            x = pack[me]
        else:
            pack_copies[k].wait_recv()
            x = got[k]
        at = pl.multiple_of(src * depth, 128)
        dims = (((1,), (1,)), ((), ()))
        t0 = lax.dot_general(x, a[:, pl.ds(at, half)], dims, preferred_element_type=F32)
        t1 = lax.dot_general(
            x, a[:, pl.ds(pl.multiple_of(at + half, 128), half)], dims, preferred_element_type=F32
        )
        low = low + t0[:CAP] + t1[CAP:]
    low = low.astype(BF16)

    u_copy.wait()
    lora_copies = [None] * LEVEL
    for k in (3, 2, 1, 0):
        dy, dc = k // 2, k % 2
        value = jnp.concatenate(
            [mm(low, u[:, feature(zz, dy, dc)]) for zz in range(levels)], axis=0
        ).astype(BF16)
        if k == 0:
            lora_in[0] = value
        else:
            lora_out[k] = value
            lora_copies[k] = send(
                lora_out.at[k], lora_in.at[k], lora_s.at[k], lora_r.at[k], device(0, dy, dc)
            )
            lora_copies[k].start()
    for k in (1, 2, 3):
        lora_copies[k].wait_recv()

    terms = lora_in[...].reshape(LEVEL * levels * CAP, width)
    places = [sel[back(0, k // 2, k % 2)] for k in range(LEVEL)]

    def summed(dz):
        zz = (z + dz) % levels
        place = jnp.concatenate(
            [jnp.where(zz == i, places[k], 0.0) for k in range(LEVEL) for i in range(levels)], axis=0
        ).astype(BF16)
        return total[zz] + lax.dot_general(
            place, terms, (((0,), (0,)), ((), ())), preferred_element_type=F32
        )

    z_copies = [None] * levels
    for dz in range(levels - 1, 0, -1):
        z_out[dz] = summed(dz).astype(BF16)
        z_copies[dz] = send(z_out.at[dz], z_in.at[dz], z_s.at[dz], z_r.at[dz], device(dz, 0, 0))
        z_copies[dz].start()
    result = summed(0)
    for dz in range(1, levels):
        z_copies[dz].wait_recv()
        result = result + z_in[dz].astype(F32)
    out[...] = result.astype(out.dtype)

    for k in range(1, parts):
        pack_copies[k].wait_send()
    for i in range(2 * levels):
        core_copy(i).wait_send()
    for i in range(levels):
        y_copy(i).wait_send()
    for k in (1, 2, 3):
        lora_copies[k].wait_send()
    for dz in range(1, levels):
        z_copies[dz].wait_send()


def fused(hidden, down_weight, adapter_down, adapter_up, ids, holder):
    parts = lax.axis_size("tp")
    levels = parts // LEVEL
    rows, depth = hidden.shape
    features = down_weight.shape[1]
    width = features // parts
    rank = adapter_down.shape[0]
    vmem = pl.BlockSpec(memory_space=pltpu.VMEM)
    anywhere = pl.BlockSpec(memory_space=pl.ANY)
    dma = pltpu.SemaphoreType.DMA
    return pl.pallas_call(
        functools.partial(kernel, levels),
        out_shape=jax.ShapeDtypeStruct((rows, width), BF16),
        in_specs=[vmem, vmem, vmem, anywhere, anywhere, anywhere],
        out_specs=vmem,
        scratch_shapes=[
            pltpu.VMEM((parts, depth, width), BF16),
            pltpu.VMEM(adapter_down.shape, BF16),
            pltpu.VMEM(adapter_up.shape, BF16),
            pltpu.VMEM((parts, CAP, rows), F32),
            pltpu.VMEM((parts, 2 * CAP, depth // 2), BF16),
            pltpu.VMEM((parts, 2 * CAP, depth // 2), BF16),
            pltpu.VMEM((2 * levels, rows, width), F32),
            pltpu.VMEM((2 * levels, rows, width), F32),
            pltpu.VMEM((levels, rows, width), BF16),
            pltpu.VMEM((levels, rows, width), BF16),
            pltpu.VMEM((levels, rows, width), F32),
            pltpu.VMEM((LEVEL, levels * CAP, width), BF16),
            pltpu.VMEM((LEVEL, levels * CAP, width), BF16),
            pltpu.VMEM((levels, rows, width), BF16),
            pltpu.VMEM((levels, rows, width), BF16),
            dma((parts,)), dma, dma,
            dma((parts,)), dma((parts,)),
            dma((2 * levels,)), dma((2 * levels,)),
            dma((levels,)), dma((levels,)),
            dma((LEVEL,)), dma((LEVEL,)),
            dma((levels,)), dma((levels,)),
        ],
        compiler_params=pltpu.CompilerParams(
            collective_id=0, has_side_effects=True, vmem_limit_bytes=60 * 1024 * 1024
        ),
        cost_estimate=pl.CostEstimate(
            flops=2 * rows * depth * features,
            bytes_accessed=2 * depth * features,
            transcendentals=0,
        ),
    )(hidden, ids.reshape(1, rows), holder.reshape(1, parts), down_weight, adapter_down, adapter_up)


def general(
    hidden, down_weight, adapter_down_weight, adapter_up_weight, row_adapter_ids, adapter_holder
):
    parts = lax.axis_size("tp")
    rows = hidden.shape[0]
    holder_device = adapter_holder[row_adapter_ids]
    owners = jnp.arange(parts, dtype=jnp.int32)
    onehot = (holder_device[:, None] == owners[None, :]).astype(jnp.int32)
    within = jnp.sum(jnp.cumsum(onehot, axis=0) * onehot, axis=1) - 1
    row_ids = jnp.arange(rows, dtype=jnp.int32)
    table = jnp.full((parts, CAP), rows, jnp.int32).at[holder_device, within].set(row_ids)
    outgoing = jnp.take(hidden, table, axis=0, mode="fill", fill_value=0)
    reduced_state = jnp.einsum(
        "sf,rf->sr",
        lax.all_to_all(outgoing, "tp", split_axis=0, concat_axis=2, tiled=True)[0],
        adapter_down_weight[0],
        preferred_element_type=F32,
    ).astype(BF16)
    mine = (holder_device == lax.axis_index("tp"))[:, None]
    low = jnp.where(mine, jnp.take(reduced_state, within, axis=0, mode="clip"), 0)
    partial_sum = mm(hidden, down_weight) + mm(low, adapter_up_weight[0])
    return lax.psum_scatter(partial_sum, "tp", scatter_dimension=1, tiled=True).astype(BF16)


def local(
    hidden, down_weight, adapter_down_weight, adapter_up_weight, row_adapter_ids, adapter_holder
):
    parts = lax.axis_size("tp")
    tiled = (
        parts % LEVEL == 0
        and hidden.shape[1] % 256 == 0
        and down_weight.shape[1] % (128 * parts) == 0
        and hidden.shape[0] == 128
        and hidden.shape[1] * down_weight.shape[1] <= 2**24
        and adapter_holder.shape[0] == parts
    )
    if tiled:
        return fused(
            hidden, down_weight, adapter_down_weight[0], adapter_up_weight[0],
            row_adapter_ids, adapter_holder,
        )
    return general(
        hidden, down_weight, adapter_down_weight, adapter_up_weight, row_adapter_ids, adapter_holder
    )


def solution(mesh):
    return jax.shard_map(
        local,
        mesh=mesh,
        in_specs=(
            P("groups", "tp"),
            P("tp", None),
            P("tp", None, None),
            P("tp", None, None),
            P("groups"),
            P(),
        ),
        out_specs=P("groups", "tp"),
        check_vma=False,
    )
```

```python
import functools

import jax
import jax.numpy as jnp
from jax import lax
from jax.experimental import pallas as pl
from jax.experimental.pallas import tpu as pltpu
from jax.sharding import PartitionSpec as P

CAP = 24
F32 = jnp.float32
BF16 = jnp.bfloat16
LEVEL = 4


def mm(a, b):
    return jnp.dot(a, b, preferred_element_type=F32)


def kernel(
    levels, hid, ids, holder, down_hbm, a_hbm, u_hbm, out,
    w, a, u, sel, place, far, near_out, near_in, relay_out, relay_in, direct_out, direct_in,
    core_out, core_in, y_out, y_in, total, lora_out, lora_in, z_out, z_in,
    w_sem, a_sem, u_sem, far_s, far_r, near_s, near_r, relay_s, relay_r, direct_s, direct_r,
    core_s, core_r, y_s, y_r, lora_s, lora_r, z_s, z_r,
):
    parts = levels * LEVEL
    side = parts // 2
    rows, depth = hid.shape
    relayed = far.shape[1]
    width = out.shape[1]
    me = lax.axis_index("tp")
    z, y, c = me // 4, (me // 2) % 2, me % 2
    half, zin = z // 2, z % 2

    def device(dz, dy, dc):
        return ((z + dz) % levels) * 4 + ((y + dy) % 2) * 2 + (c + dc) % 2

    def back(dz, dy, dc):
        return ((z + levels - dz) % levels) * 4 + ((y + dy) % 2) * 2 + (c + dc) % 2

    def inner(j):
        return ((zin + j // 4) % 2) * 4 + ((y + (j // 2) % 2) % 2) * 2 + (c + j % 2) % 2

    def feature(zz, dy, dc):
        block = zz * 4 + ((y + dy) % 2) * 2 + (c + dc) % 2
        return pl.ds(pl.multiple_of(block * width, 128), width)

    def send(src, dst, s, r, dev):
        return pltpu.make_async_remote_copy(
            src_ref=src, dst_ref=dst, send_sem=s, recv_sem=r,
            device_id={"tp": dev}, device_id_type=pl.DeviceIdType.MESH,
        )

    phases = [(1, 1), (1, 0), (0, 1), (0, 0)]

    def w_copy(p, zz):
        dy, dc = phases[p]
        return pltpu.make_async_copy(
            down_hbm.at[:, feature(zz, dy, dc)], w.at[p * levels + zz], w_sem.at[p * levels + zz]
        )

    barrier = pltpu.get_barrier_semaphore()
    offsets = [(k // 4, (k // 2) % 2, k % 2) for k in range(parts)]
    for k in range(1, parts):
        pl.semaphore_signal(
            barrier, inc=1, device_id={"tp": device(*offsets[k])},
            device_id_type=pl.DeviceIdType.MESH,
        )
    for p in range(4):
        for zz in range(levels):
            w_copy(p, zz).start()
    a_copy = pltpu.make_async_copy(a_hbm, a, a_sem)
    u_copy = pltpu.make_async_copy(u_hbm, u, u_sem)
    a_copy.start()
    u_copy.start()

    held = (holder[...] == lax.broadcasted_iota(jnp.int32, (parts, parts), 0)).astype(F32)
    named = (ids[...] == lax.broadcasted_iota(jnp.int32, (parts, rows), 0)).astype(F32)
    owned = mm(held.astype(BF16), named.astype(BF16))
    upto = (
        lax.broadcasted_iota(jnp.int32, (rows, rows), 0)
        <= lax.broadcasted_iota(jnp.int32, (rows, rows), 1)
    ).astype(F32)
    count = mm(owned.astype(BF16), upto.astype(BF16))
    slot = jnp.where(owned > 0.5, count - 1.0, -1.0).astype(jnp.int32)
    for o in range(parts):
        sel[o] = (
            slot[o : o + 1, :] == lax.broadcasted_iota(jnp.int32, (CAP, rows), 0)
        ).astype(F32)

    pl.semaphore_wait(barrier, parts - 1)
    far_copy = send(hid.at[:, pl.ds(0, relayed)], far, far_s, far_r, device(levels // 2, 0, 0))
    far_copy.start()

    def pack(first, groups, x, to):
        def body(i, carry):
            s = sel[pl.ds(first + i * 4, 4)].reshape(4 * CAP, rows).astype(BF16)
            t = mm(s, x())
            n = t.shape[1] // 2
            for j in range(4):
                r = t[j * CAP : (j + 1) * CAP]
                to[i * 4 + j] = jnp.concatenate([r[:, :n], r[:, n:]], axis=0).astype(BF16)
            return carry

        lax.fori_loop(0, groups, body, 0)

    pack(half * side, side // 4, lambda: hid[:, :relayed], near_out)
    near_copies = [
        send(near_out.at[inner(j)], near_in.at[j], near_s.at[j], near_r.at[j], half * side + inner(j))
        for j in range(side)
    ]
    for j in range(side - 1, 0, -1):
        near_copies[j].start()
    pack(0, levels, lambda: hid[:, relayed:], direct_out)
    direct_copies = [
        send(direct_out.at[device(*offsets[k])], direct_in.at[k], direct_s.at[k], direct_r.at[k],
             device(*offsets[k]))
        for k in range(parts)
    ]
    for k in range(parts - 1, 0, -1):
        direct_copies[k].start()

    def core_copy(i):
        return send(core_out.at[i], core_in.at[i], core_s.at[i], core_r.at[i], device(0, 0, 1))

    def y_copy(i):
        return send(y_out.at[i], y_in.at[i], y_s.at[i], y_r.at[i], device(0, 1, 0))

    def product(p, zz):
        w_copy(p, zz).wait()
        return mm(hid[...], w[p * levels + zz])

    def to_core(base, p):
        def body(zz, carry):
            core_out[base + zz] = product(p, zz)
            core_copy(base + zz).start()
            return carry
        lax.fori_loop(0, levels, body, 0)

    def to_y(zz, carry):
        t = product(1, zz)
        core_copy(zz).wait_recv()
        y_out[zz] = (t + core_in[zz]).astype(BF16)
        y_copy(zz).start()
        return carry

    def keep(zz, carry):
        t = product(3, zz)
        core_copy(levels + zz).wait_recv()
        t = t + core_in[levels + zz]
        y_copy(zz).wait_recv()
        total[zz] = t + y_in[zz].astype(F32)
        return carry

    to_core(0, 0)
    lax.fori_loop(0, levels, to_y, 0)
    to_core(levels, 2)

    far_copy.wait_recv()
    pack(half * side, side // 4, lambda: far[...], relay_out)
    relay_copies = [
        send(relay_out.at[inner(j)], relay_in.at[j], relay_s.at[j], relay_r.at[j],
             half * side + inner(j))
        for j in range(side)
    ]
    for j in range(side - 1, 0, -1):
        relay_copies[j].start()

    lax.fori_loop(0, levels, keep, 0)

    level_sel = [sel[back(0, k // 2, k % 2)] for k in range(LEVEL)]
    zeros = jnp.zeros((CAP, rows), F32)
    for pos in range(2):
        pieces = []
        for s in level_sel:
            pieces += [s, zeros] if pos == 0 else [zeros, s]
        place[pos] = jnp.concatenate(pieces, axis=0).T.astype(BF16)

    a_copy.wait()

    def down_map(x, at):
        n = x.shape[1]
        dims = (((1,), (1,)), ((), ()))
        t0 = lax.dot_general(
            x, a[:, pl.ds(pl.multiple_of(at, 128), n)], dims, preferred_element_type=F32
        )
        t1 = lax.dot_general(
            x, a[:, pl.ds(pl.multiple_of(at + n, 128), n)], dims, preferred_element_type=F32
        )
        return t0[:CAP] + t1[CAP:]

    low = down_map(near_out[inner(0)], me * depth)
    low += down_map(direct_out[me], me * depth + relayed)
    low += down_map(relay_out[inner(0)], ((1 - half) * side + inner(0)) * depth)
    for j in range(1, side):
        near_copies[j].wait_recv()
        low += down_map(near_in[j], (half * side + inner(j)) * depth)
    for k in range(1, parts):
        direct_copies[k].wait_recv()
        low += down_map(direct_in[k], back(*offsets[k]) * depth + relayed)
    for j in range(1, side):
        relay_copies[j].wait_recv()
        low += down_map(relay_in[j], ((1 - half) * side + inner(j)) * depth)
    low = low.astype(BF16)

    u_copy.wait()
    steps = [(2, 3), (1, 0)]
    lora_copies = {}
    for piece, dzs in enumerate(steps):
        for k in (3, 2, 1, 0):
            dy, dc = k // 2, k % 2
            value = jnp.concatenate(
                [mm(low, u[:, feature((z + dz) % levels, dy, dc)]) for dz in dzs], axis=0
            ).astype(BF16)
            i = piece * LEVEL + k
            if k == 0:
                lora_in[i] = value
            else:
                lora_out[i] = value
                lora_copies[i] = send(
                    lora_out.at[i], lora_in.at[i], lora_s.at[i], lora_r.at[i], device(0, dy, dc)
                )
                lora_copies[i].start()

    z_copies = {}
    for piece, dzs in enumerate(steps):
        for k in (1, 2, 3):
            lora_copies[piece * LEVEL + k].wait_recv()
        terms = lora_in[piece * LEVEL : (piece + 1) * LEVEL].reshape(LEVEL * 2 * CAP, width)
        for pos, dz in enumerate(dzs):
            t = total[(z + dz) % levels] + mm(place[pos], terms)
            if dz == 0:
                result = t
            else:
                z_out[dz] = t.astype(BF16)
                z_copies[dz] = send(
                    z_out.at[dz], z_in.at[dz], z_s.at[dz], z_r.at[dz], device(dz, 0, 0)
                )
                z_copies[dz].start()
    for dz in range(1, levels):
        z_copies[dz].wait_recv()
        result = result + z_in[dz].astype(F32)
    out[...] = result.astype(out.dtype)

    far_copy.wait_send()
    for j in range(1, side):
        near_copies[j].wait_send()
        relay_copies[j].wait_send()
    for k in range(1, parts):
        direct_copies[k].wait_send()
    for i in range(2 * levels):
        core_copy(i).wait_send()
    for i in range(levels):
        y_copy(i).wait_send()
    for i in lora_copies:
        lora_copies[i].wait_send()
    for dz in range(1, levels):
        z_copies[dz].wait_send()


def fused(hidden, down_weight, adapter_down, adapter_up, ids, holder):
    parts = lax.axis_size("tp")
    levels = parts // LEVEL
    rows, depth = hidden.shape
    features = down_weight.shape[1]
    width = features // parts
    relayed = depth // 256 * 4 // 7 * 256
    direct = depth - relayed
    side = parts // 2
    vmem = pl.BlockSpec(memory_space=pltpu.VMEM)
    anywhere = pl.BlockSpec(memory_space=pl.ANY)
    dma = pltpu.SemaphoreType.DMA
    return pl.pallas_call(
        functools.partial(kernel, levels),
        out_shape=jax.ShapeDtypeStruct((rows, width), BF16),
        in_specs=[vmem, vmem, vmem, anywhere, anywhere, anywhere],
        out_specs=vmem,
        scratch_shapes=[
            pltpu.VMEM((parts, depth, width), BF16),
            pltpu.VMEM(adapter_down.shape, BF16),
            pltpu.VMEM(adapter_up.shape, BF16),
            pltpu.VMEM((parts, CAP, rows), F32),
            pltpu.VMEM((2, rows, LEVEL * 2 * CAP), BF16),
            pltpu.VMEM((rows, relayed), BF16),
            pltpu.VMEM((side, 2 * CAP, relayed // 2), BF16),
            pltpu.VMEM((side, 2 * CAP, relayed // 2), BF16),
            pltpu.VMEM((side, 2 * CAP, relayed // 2), BF16),
            pltpu.VMEM((side, 2 * CAP, relayed // 2), BF16),
            pltpu.VMEM((parts, 2 * CAP, direct // 2), BF16),
            pltpu.VMEM((parts, 2 * CAP, direct // 2), BF16),
            pltpu.VMEM((2 * levels, rows, width), F32),
            pltpu.VMEM((2 * levels, rows, width), F32),
            pltpu.VMEM((levels, rows, width), BF16),
            pltpu.VMEM((levels, rows, width), BF16),
            pltpu.VMEM((levels, rows, width), F32),
            pltpu.VMEM((2 * LEVEL, 2 * CAP, width), BF16),
            pltpu.VMEM((2 * LEVEL, 2 * CAP, width), BF16),
            pltpu.VMEM((levels, rows, width), BF16),
            pltpu.VMEM((levels, rows, width), BF16),
            dma((parts,)), dma, dma,
            dma, dma,
            dma((side,)), dma((side,)),
            dma((side,)), dma((side,)),
            dma((parts,)), dma((parts,)),
            dma((2 * levels,)), dma((2 * levels,)),
            dma((levels,)), dma((levels,)),
            dma((2 * LEVEL,)), dma((2 * LEVEL,)),
            dma((levels,)), dma((levels,)),
        ],
        compiler_params=pltpu.CompilerParams(
            collective_id=0, has_side_effects=True, vmem_limit_bytes=60 * 1024 * 1024
        ),
        cost_estimate=pl.CostEstimate(
            flops=2 * rows * depth * features,
            bytes_accessed=2 * depth * features,
            transcendentals=0,
        ),
    )(hidden, ids.reshape(1, rows), holder.reshape(1, parts), down_weight, adapter_down, adapter_up)


def general(
    hidden, down_weight, adapter_down_weight, adapter_up_weight, row_adapter_ids, adapter_holder
):
    parts = lax.axis_size("tp")
    rows = hidden.shape[0]
    holder_device = adapter_holder[row_adapter_ids]
    owners = jnp.arange(parts, dtype=jnp.int32)
    onehot = (holder_device[:, None] == owners[None, :]).astype(jnp.int32)
    within = jnp.sum(jnp.cumsum(onehot, axis=0) * onehot, axis=1) - 1
    row_ids = jnp.arange(rows, dtype=jnp.int32)
    table = jnp.full((parts, CAP), rows, jnp.int32).at[holder_device, within].set(row_ids)
    outgoing = jnp.take(hidden, table, axis=0, mode="fill", fill_value=0)
    reduced_state = jnp.einsum(
        "sf,rf->sr",
        lax.all_to_all(outgoing, "tp", split_axis=0, concat_axis=2, tiled=True)[0],
        adapter_down_weight[0],
        preferred_element_type=F32,
    ).astype(BF16)
    mine = (holder_device == lax.axis_index("tp"))[:, None]
    low = jnp.where(mine, jnp.take(reduced_state, within, axis=0, mode="clip"), 0)
    partial_sum = mm(hidden, down_weight) + mm(low, adapter_up_weight[0])
    return lax.psum_scatter(partial_sum, "tp", scatter_dimension=1, tiled=True).astype(BF16)


def local(
    hidden, down_weight, adapter_down_weight, adapter_up_weight, row_adapter_ids, adapter_holder
):
    parts = lax.axis_size("tp")
    tiled = (
        parts == 4 * LEVEL
        and hidden.shape[1] % 256 == 0
        and down_weight.shape[1] % (128 * parts) == 0
        and hidden.shape[0] == 128
        and hidden.shape[1] * down_weight.shape[1] <= 2**24
        and adapter_holder.shape[0] == parts
    )
    if tiled:
        return fused(
            hidden, down_weight, adapter_down_weight[0], adapter_up_weight[0],
            row_adapter_ids, adapter_holder,
        )
    return general(
        hidden, down_weight, adapter_down_weight, adapter_up_weight, row_adapter_ids, adapter_holder
    )


def solution(mesh):
    return jax.shard_map(
        local,
        mesh=mesh,
        in_specs=(
            P("groups", "tp"),
            P("tp", None),
            P("tp", None, None),
            P("tp", None, None),
            P("groups"),
            P(),
        ),
        out_specs=P("groups", "tp"),
        check_vma=False,
    )
```

```python
import functools

import jax
import jax.numpy as jnp
from jax import lax
from jax.experimental import pallas as pl
from jax.experimental.pallas import tpu as pltpu
from jax.sharding import PartitionSpec as P

CAP = 24
F32 = jnp.float32
BF16 = jnp.bfloat16
LEVEL = 4


def mm(a, b):
    return jnp.dot(a, b, preferred_element_type=F32)


def kernel(
    levels, hid, ids, holder, down_hbm, a_hbm, u_hbm, out,
    w, a, u, sel, place, far, aside, near_out, near_in, relay_out, relay_in, direct_out, direct_in,
    core_out, core_in, y_out, y_in, total, lora_out, lora_in, z_out, z_in,
    w_sem, a_sem, u_sem, far_s, far_r, aside_s, aside_r, near_s, near_r, relay_s, relay_r, direct_s, direct_r,
    core_s, core_r, y_s, y_r, lora_s, lora_r, z_s, z_r,
):
    parts = levels * LEVEL
    side = parts // 2
    rows, depth = hid.shape
    relayed = far.shape[1]
    width = out.shape[1]
    me = lax.axis_index("tp")
    z, y, c = me // 4, (me // 2) % 2, me % 2
    half, zin = z // 2, z % 2

    def device(dz, dy, dc):
        return ((z + dz) % levels) * 4 + ((y + dy) % 2) * 2 + (c + dc) % 2

    def back(dz, dy, dc):
        return ((z + levels - dz) % levels) * 4 + ((y + dy) % 2) * 2 + (c + dc) % 2

    def inner(j):
        return ((zin + j // 4) % 2) * 4 + ((y + (j // 2) % 2) % 2) * 2 + (c + j % 2) % 2

    def feature(zz, dy, dc):
        block = zz * 4 + ((y + dy) % 2) * 2 + (c + dc) % 2
        return pl.ds(pl.multiple_of(block * width, 128), width)

    def send(src, dst, s, r, dev):
        return pltpu.make_async_remote_copy(
            src_ref=src, dst_ref=dst, send_sem=s, recv_sem=r,
            device_id={"tp": dev}, device_id_type=pl.DeviceIdType.MESH,
        )

    phases = [(1, 1), (1, 0), (0, 1), (0, 0)]

    def w_copy(p, zz):
        dy, dc = phases[p]
        return pltpu.make_async_copy(
            down_hbm.at[:, feature(zz, dy, dc)], w.at[p * levels + zz], w_sem.at[p * levels + zz]
        )

    barrier = pltpu.get_barrier_semaphore()
    offsets = [(k // 4, (k // 2) % 2, k % 2) for k in range(parts)]
    for k in range(1, parts):
        pl.semaphore_signal(
            barrier, inc=1, device_id={"tp": device(*offsets[k])},
            device_id_type=pl.DeviceIdType.MESH,
        )
    for p in range(4):
        for zz in range(levels):
            w_copy(p, zz).start()
    a_copy = pltpu.make_async_copy(a_hbm, a, a_sem)
    u_copy = pltpu.make_async_copy(u_hbm, u, u_sem)
    a_copy.start()
    u_copy.start()

    held = (holder[...] == lax.broadcasted_iota(jnp.int32, (parts, parts), 0)).astype(F32)
    named = (ids[...] == lax.broadcasted_iota(jnp.int32, (parts, rows), 0)).astype(F32)
    owned = mm(held.astype(BF16), named.astype(BF16))
    upto = (
        lax.broadcasted_iota(jnp.int32, (rows, rows), 0)
        <= lax.broadcasted_iota(jnp.int32, (rows, rows), 1)
    ).astype(F32)
    count = mm(owned.astype(BF16), upto.astype(BF16))
    slot = jnp.where(owned > 0.5, count - 1.0, -1.0).astype(jnp.int32)
    for o in range(parts):
        sel[o] = (
            slot[o : o + 1, :] == lax.broadcasted_iota(jnp.int32, (CAP, rows), 0)
        ).astype(F32)

    pl.semaphore_wait(barrier, parts - 1)
    far_copy = send(hid.at[:, pl.ds(0, relayed)], far, far_s, far_r, device(levels // 2, 0, 0))
    far_copy.start()
    aside_copy = send(hid.at[:, pl.ds(relayed, depth - relayed)], aside, aside_s, aside_r, device(0, 1, 0))
    aside_copy.start()

    def pack(first, groups, x, to):
        def body(i, carry):
            s = sel[pl.ds(first + i * 4, 4)].reshape(4 * CAP, rows).astype(BF16)
            t = mm(s, x())
            n = t.shape[1] // 2
            for j in range(4):
                r = t[j * CAP : (j + 1) * CAP]
                to[i * 4 + j] = jnp.concatenate([r[:, :n], r[:, n:]], axis=0).astype(BF16)
            return carry

        lax.fori_loop(0, groups, body, 0)

    pack(half * side, side // 4, lambda: hid[:, :relayed], near_out)
    near_copies = [
        send(near_out.at[inner(j)], near_in.at[j], near_s.at[j], near_r.at[j], half * side + inner(j))
        for j in range(side)
    ]
    for j in range(side - 1, 0, -1):
        near_copies[j].start()
    def core_copy(i):
        return send(core_out.at[i], core_in.at[i], core_s.at[i], core_r.at[i], device(0, 0, 1))

    def y_copy(i):
        return send(y_out.at[i], y_in.at[i], y_s.at[i], y_r.at[i], device(0, 1, 0))

    def product(p, zz):
        w_copy(p, zz).wait()
        return mm(hid[...], w[p * levels + zz])

    def to_core(base, p):
        def body(zz, carry):
            core_out[base + zz] = product(p, zz)
            core_copy(base + zz).start()
            return carry
        lax.fori_loop(0, levels, body, 0)

    def to_y(zz, carry):
        t = product(1, zz)
        core_copy(zz).wait_recv()
        y_out[zz] = (t + core_in[zz]).astype(BF16)
        y_copy(zz).start()
        return carry

    def keep(zz, carry):
        t = product(3, zz)
        core_copy(levels + zz).wait_recv()
        t = t + core_in[levels + zz]
        total[zz] = t
        return carry

    to_core(0, 0)
    lax.fori_loop(0, levels, to_y, 0)
    aside_copy.wait_recv()

    def pack_direct(i, carry):
        s = sel[pl.ds(i * 4 + y * 2, 2)].reshape(2 * CAP, rows).astype(BF16)
        t = mm(s, hid[:, relayed:])
        v = mm(s, aside[...])
        for j in range(2):
            at = slice(j * CAP, (j + 1) * CAP)
            direct_out[i * 2 + j] = jnp.concatenate([t[at], v[at]], axis=0).astype(BF16)
        return carry

    lax.fori_loop(0, levels, pack_direct, 0)
    direct_copies = []
    for k in range(side):
        dev = device(k // 2, 0, k % 2)
        direct_copies.append(
            send(direct_out.at[dev // 4 * 2 + dev % 2], direct_in.at[k], direct_s.at[k],
                 direct_r.at[k], dev)
        )
    for k in range(side - 1, 0, -1):
        direct_copies[k].start()

    to_core(levels, 2)

    far_copy.wait_recv()
    pack(half * side, side // 4, lambda: far[...], relay_out)
    relay_copies = [
        send(relay_out.at[inner(j)], relay_in.at[j], relay_s.at[j], relay_r.at[j],
             half * side + inner(j))
        for j in range(side)
    ]
    for j in range(side - 1, 0, -1):
        relay_copies[j].start()

    lax.fori_loop(0, levels, keep, 0)

    level_sel = [sel[back(0, k // 2, k % 2)] for k in range(LEVEL)]
    zeros = jnp.zeros((CAP, rows), F32)
    for pos in range(2):
        pieces = []
        for s in level_sel:
            pieces += [s, zeros] if pos == 0 else [zeros, s]
        place[pos] = jnp.concatenate(pieces, axis=0).T.astype(BF16)

    a_copy.wait()

    def down_map(x, at):
        n = x.shape[1]
        dims = (((1,), (1,)), ((), ()))
        t0 = lax.dot_general(
            x, a[:, pl.ds(pl.multiple_of(at, 128), n)], dims, preferred_element_type=F32
        )
        t1 = lax.dot_general(
            x, a[:, pl.ds(pl.multiple_of(at + n, 128), n)], dims, preferred_element_type=F32
        )
        return t0[:CAP] + t1[CAP:]

    low = down_map(near_out[inner(0)], me * depth)

    def direct_map(x, src, pair):
        dims = (((1,), (1,)), ((), ()))
        n = x.shape[1]
        t0 = lax.dot_general(
            x, a[:, pl.ds(pl.multiple_of(src * depth + relayed, 128), n)], dims,
            preferred_element_type=F32,
        )
        t1 = lax.dot_general(
            x, a[:, pl.ds(pl.multiple_of(pair * depth + relayed, 128), n)], dims,
            preferred_element_type=F32,
        )
        return t0[:CAP] + t1[CAP:]

    low += direct_map(direct_out[z * 2 + c], me, device(0, 1, 0))
    low += down_map(relay_out[inner(0)], ((1 - half) * side + inner(0)) * depth)
    for j in range(1, side):
        near_copies[j].wait_recv()
        low += down_map(near_in[j], (half * side + inner(j)) * depth)
    for k in range(1, side):
        direct_copies[k].wait_recv()
        low += direct_map(direct_in[k], back(k // 2, 0, k % 2), back(k // 2, 1, k % 2))
    for j in range(1, side):
        relay_copies[j].wait_recv()
        low += down_map(relay_in[j], ((1 - half) * side + inner(j)) * depth)
    low = low.astype(BF16)

    u_copy.wait()
    steps = [(2, 3), (1, 0)]
    lora_copies = {}
    for piece, dzs in enumerate(steps):
        for k in (3, 2, 1, 0):
            dy, dc = k // 2, k % 2
            value = jnp.concatenate(
                [mm(low, u[:, feature((z + dz) % levels, dy, dc)]) for dz in dzs], axis=0
            ).astype(BF16)
            i = piece * LEVEL + k
            if k == 0:
                lora_in[i] = value
            else:
                lora_out[i] = value
                lora_copies[i] = send(
                    lora_out.at[i], lora_in.at[i], lora_s.at[i], lora_r.at[i], device(0, dy, dc)
                )
                lora_copies[i].start()

    z_copies = {}
    for piece, dzs in enumerate(steps):
        for k in (1, 2, 3):
            lora_copies[piece * LEVEL + k].wait_recv()
        terms = lora_in[piece * LEVEL : (piece + 1) * LEVEL].reshape(LEVEL * 2 * CAP, width)
        for pos, dz in enumerate(dzs):
            zz = (z + dz) % levels
            y_copy(zz).wait_recv()
            t = total[zz] + y_in[zz].astype(F32) + mm(place[pos], terms)
            if dz == 0:
                result = t
            else:
                z_out[dz] = t.astype(BF16)
                z_copies[dz] = send(
                    z_out.at[dz], z_in.at[dz], z_s.at[dz], z_r.at[dz], device(dz, 0, 0)
                )
                z_copies[dz].start()
    for dz in range(1, levels):
        z_copies[dz].wait_recv()
        result = result + z_in[dz].astype(F32)
    out[...] = result.astype(out.dtype)

    far_copy.wait_send()
    for j in range(1, side):
        near_copies[j].wait_send()
        relay_copies[j].wait_send()
    aside_copy.wait_send()
    for k in range(1, side):
        direct_copies[k].wait_send()
    for i in range(2 * levels):
        core_copy(i).wait_send()
    for i in range(levels):
        y_copy(i).wait_send()
    for i in lora_copies:
        lora_copies[i].wait_send()
    for dz in range(1, levels):
        z_copies[dz].wait_send()


def fused(hidden, down_weight, adapter_down, adapter_up, ids, holder):
    parts = lax.axis_size("tp")
    levels = parts // LEVEL
    rows, depth = hidden.shape
    features = down_weight.shape[1]
    width = features // parts
    relayed = depth // 256 * 4 // 7 * 256
    direct = depth - relayed
    side = parts // 2
    vmem = pl.BlockSpec(memory_space=pltpu.VMEM)
    anywhere = pl.BlockSpec(memory_space=pl.ANY)
    dma = pltpu.SemaphoreType.DMA
    return pl.pallas_call(
        functools.partial(kernel, levels),
        out_shape=jax.ShapeDtypeStruct((rows, width), BF16),
        in_specs=[vmem, vmem, vmem, anywhere, anywhere, anywhere],
        out_specs=vmem,
        scratch_shapes=[
            pltpu.VMEM((parts, depth, width), BF16),
            pltpu.VMEM(adapter_down.shape, BF16),
            pltpu.VMEM(adapter_up.shape, BF16),
            pltpu.VMEM((parts, CAP, rows), F32),
            pltpu.VMEM((2, rows, LEVEL * 2 * CAP), BF16),
            pltpu.VMEM((rows, relayed), BF16),
            pltpu.VMEM((rows, direct), BF16),
            pltpu.VMEM((side, 2 * CAP, relayed // 2), BF16),
            pltpu.VMEM((side, 2 * CAP, relayed // 2), BF16),
            pltpu.VMEM((side, 2 * CAP, relayed // 2), BF16),
            pltpu.VMEM((side, 2 * CAP, relayed // 2), BF16),
            pltpu.VMEM((side, 2 * CAP, direct), BF16),
            pltpu.VMEM((side, 2 * CAP, direct), BF16),
            pltpu.VMEM((2 * levels, rows, width), F32),
            pltpu.VMEM((2 * levels, rows, width), F32),
            pltpu.VMEM((levels, rows, width), BF16),
            pltpu.VMEM((levels, rows, width), BF16),
            pltpu.VMEM((levels, rows, width), F32),
            pltpu.VMEM((2 * LEVEL, 2 * CAP, width), BF16),
            pltpu.VMEM((2 * LEVEL, 2 * CAP, width), BF16),
            pltpu.VMEM((levels, rows, width), BF16),
            pltpu.VMEM((levels, rows, width), BF16),
            dma((parts,)), dma, dma,
            dma, dma,
            dma, dma,
            dma((side,)), dma((side,)),
            dma((side,)), dma((side,)),
            dma((side,)), dma((side,)),
            dma((2 * levels,)), dma((2 * levels,)),
            dma((levels,)), dma((levels,)),
            dma((2 * LEVEL,)), dma((2 * LEVEL,)),
            dma((levels,)), dma((levels,)),
        ],
        compiler_params=pltpu.CompilerParams(
            collective_id=0, has_side_effects=True, vmem_limit_bytes=60 * 1024 * 1024
        ),
        cost_estimate=pl.CostEstimate(
            flops=2 * rows * depth * features,
            bytes_accessed=2 * depth * features,
            transcendentals=0,
        ),
    )(hidden, ids.reshape(1, rows), holder.reshape(1, parts), down_weight, adapter_down, adapter_up)


def general(
    hidden, down_weight, adapter_down_weight, adapter_up_weight, row_adapter_ids, adapter_holder
):
    parts = lax.axis_size("tp")
    rows = hidden.shape[0]
    holder_device = adapter_holder[row_adapter_ids]
    owners = jnp.arange(parts, dtype=jnp.int32)
    onehot = (holder_device[:, None] == owners[None, :]).astype(jnp.int32)
    within = jnp.sum(jnp.cumsum(onehot, axis=0) * onehot, axis=1) - 1
    row_ids = jnp.arange(rows, dtype=jnp.int32)
    table = jnp.full((parts, CAP), rows, jnp.int32).at[holder_device, within].set(row_ids)
    outgoing = jnp.take(hidden, table, axis=0, mode="fill", fill_value=0)
    reduced_state = jnp.einsum(
        "sf,rf->sr",
        lax.all_to_all(outgoing, "tp", split_axis=0, concat_axis=2, tiled=True)[0],
        adapter_down_weight[0],
        preferred_element_type=F32,
    ).astype(BF16)
    mine = (holder_device == lax.axis_index("tp"))[:, None]
    low = jnp.where(mine, jnp.take(reduced_state, within, axis=0, mode="clip"), 0)
    partial_sum = mm(hidden, down_weight) + mm(low, adapter_up_weight[0])
    return lax.psum_scatter(partial_sum, "tp", scatter_dimension=1, tiled=True).astype(BF16)


def local(
    hidden, down_weight, adapter_down_weight, adapter_up_weight, row_adapter_ids, adapter_holder
):
    parts = lax.axis_size("tp")
    tiled = (
        parts == 4 * LEVEL
        and hidden.shape[1] % 256 == 0
        and down_weight.shape[1] % (128 * parts) == 0
        and hidden.shape[0] == 128
        and hidden.shape[1] * down_weight.shape[1] <= 2**24
        and adapter_holder.shape[0] == parts
    )
    if tiled:
        return fused(
            hidden, down_weight, adapter_down_weight[0], adapter_up_weight[0],
            row_adapter_ids, adapter_holder,
        )
    return general(
        hidden, down_weight, adapter_down_weight, adapter_up_weight, row_adapter_ids, adapter_holder
    )


def solution(mesh):
    return jax.shard_map(
        local,
        mesh=mesh,
        in_specs=(
            P("groups", "tp"),
            P("tp", None),
            P("tp", None, None),
            P("tp", None, None),
            P("groups"),
            P(),
        ),
        out_specs=P("groups", "tp"),
        check_vma=False,
    )
```

```python
import functools

import jax
import jax.numpy as jnp
from jax import lax
from jax.experimental import pallas as pl
from jax.experimental.pallas import tpu as pltpu
from jax.sharding import PartitionSpec as P

CAP = 24
F32 = jnp.float32
BF16 = jnp.bfloat16
LEVEL = 4


def mm(a, b):
    return jnp.dot(a, b, preferred_element_type=F32)


def kernel(
    levels, hid, ids, holder, down_hbm, a_hbm, u_hbm, out,
    w, a, u, sel, place, far, aside, near_out, near_in, relay_out, relay_in, direct_out, direct_in,
    core_out, core_in, y_out, y_in, total, lora_out, lora_in, z_out, z_in,
    w_sem, a_sem, u_sem, far_s, far_r, aside_s, aside_r, near_s, near_r, relay_s, relay_r, direct_s, direct_r,
    core_s, core_r, y_s, y_r, lora_s, lora_r, z_s, z_r,
):
    parts = levels * LEVEL
    side = parts // 2
    rows, depth = hid.shape
    relayed = far.shape[1]
    width = out.shape[1]
    me = lax.axis_index("tp")
    z, y, c = me // 4, (me // 2) % 2, me % 2
    half, zin = z // 2, z % 2

    def device(dz, dy, dc):
        return ((z + dz) % levels) * 4 + ((y + dy) % 2) * 2 + (c + dc) % 2

    def back(dz, dy, dc):
        return ((z + levels - dz) % levels) * 4 + ((y + dy) % 2) * 2 + (c + dc) % 2

    def inner(j):
        return ((zin + j // 4) % 2) * 4 + ((y + (j // 2) % 2) % 2) * 2 + (c + j % 2) % 2

    def feature(zz, dy, dc):
        block = zz * 4 + ((y + dy) % 2) * 2 + (c + dc) % 2
        return pl.ds(pl.multiple_of(block * width, 128), width)

    def send(src, dst, s, r, dev):
        return pltpu.make_async_remote_copy(
            src_ref=src, dst_ref=dst, send_sem=s, recv_sem=r,
            device_id={"tp": dev}, device_id_type=pl.DeviceIdType.MESH,
        )

    phases = [(1, 1), (1, 0), (0, 1), (0, 0)]

    def w_copy(p, zz):
        dy, dc = phases[p]
        return pltpu.make_async_copy(
            down_hbm.at[:, feature(zz, dy, dc)], w.at[p * levels + zz], w_sem.at[p * levels + zz]
        )

    barrier = pltpu.get_barrier_semaphore()
    peers = [device(k // 2, 0, k % 2) for k in range(side - 1, 0, -1)]
    peers += [half * side + inner(j) for j in range(side) if j // 2 % 2 == 1]
    for peer in peers:
        pl.semaphore_signal(
            barrier, inc=1, device_id={"tp": peer}, device_id_type=pl.DeviceIdType.MESH
        )
    for p in range(4):
        for zz in range(levels):
            w_copy(p, zz).start()
    a_copy = pltpu.make_async_copy(a_hbm, a, a_sem)
    u_copy = pltpu.make_async_copy(u_hbm, u, u_sem)
    a_copy.start()
    u_copy.start()

    held = (holder[...] == lax.broadcasted_iota(jnp.int32, (parts, parts), 0)).astype(F32)
    named = (ids[...] == lax.broadcasted_iota(jnp.int32, (parts, rows), 0)).astype(F32)
    owned = mm(held.astype(BF16), named.astype(BF16))
    upto = (
        lax.broadcasted_iota(jnp.int32, (rows, rows), 0)
        <= lax.broadcasted_iota(jnp.int32, (rows, rows), 1)
    ).astype(F32)
    count = mm(owned.astype(BF16), upto.astype(BF16))
    slot = jnp.where(owned > 0.5, count - 1.0, -1.0).astype(jnp.int32)
    for o in range(parts):
        sel[o] = (
            slot[o : o + 1, :] == lax.broadcasted_iota(jnp.int32, (CAP, rows), 0)
        ).astype(F32)

    pl.semaphore_wait(barrier, len(peers))
    far_copy = send(hid.at[:, pl.ds(0, relayed)], far, far_s, far_r, device(levels // 2, 0, 0))
    far_copy.start()
    aside_copy = send(hid.at[:, pl.ds(relayed, depth - relayed)], aside, aside_s, aside_r, device(0, 1, 0))
    aside_copy.start()

    def pack(first, groups, x, to):
        def body(i, carry):
            s = sel[pl.ds(first + i * 4, 4)].reshape(4 * CAP, rows).astype(BF16)
            t = mm(s, x())
            n = t.shape[1] // 2
            for j in range(4):
                r = t[j * CAP : (j + 1) * CAP]
                to[i * 4 + j] = jnp.concatenate([r[:, :n], r[:, n:]], axis=0).astype(BF16)
            return carry

        lax.fori_loop(0, groups, body, 0)

    pack(half * side, side // 4, lambda: hid[:, :relayed], near_out)
    near_copies = [
        send(near_out.at[inner(j)], near_in.at[j], near_s.at[j], near_r.at[j], half * side + inner(j))
        for j in range(side)
    ]
    for j in range(side - 1, 0, -1):
        near_copies[j].start()
    def core_copy(i):
        return send(core_out.at[i], core_in.at[i], core_s.at[i], core_r.at[i], device(0, 0, 1))

    def y_copy(i):
        return send(y_out.at[i], y_in.at[i], y_s.at[i], y_r.at[i], device(0, 1, 0))

    def product(p, zz):
        w_copy(p, zz).wait()
        return mm(hid[...], w[p * levels + zz])

    def to_core(base, p):
        def body(zz, carry):
            core_out[base + zz] = product(p, zz)
            core_copy(base + zz).start()
            return carry
        lax.fori_loop(0, levels, body, 0)

    def to_y(zz, carry):
        t = product(1, zz)
        core_copy(zz).wait_recv()
        y_out[zz] = (t + core_in[zz]).astype(BF16)
        y_copy(zz).start()
        return carry

    def keep(zz, carry):
        t = product(3, zz)
        core_copy(levels + zz).wait_recv()
        t = t + core_in[levels + zz]
        total[zz] = t
        return carry

    to_core(0, 0)
    lax.fori_loop(0, levels, to_y, 0)
    aside_copy.wait_recv()

    def pack_direct(i, carry):
        s = sel[pl.ds(i * 4 + y * 2, 2)].reshape(2 * CAP, rows).astype(BF16)
        t = mm(s, hid[:, relayed:])
        v = mm(s, aside[...])
        for j in range(2):
            at = slice(j * CAP, (j + 1) * CAP)
            direct_out[i * 2 + j] = jnp.concatenate([t[at], v[at]], axis=0).astype(BF16)
        return carry

    lax.fori_loop(0, levels, pack_direct, 0)
    direct_copies = []
    for k in range(side):
        dev = device(k // 2, 0, k % 2)
        direct_copies.append(
            send(direct_out.at[dev // 4 * 2 + dev % 2], direct_in.at[k], direct_s.at[k],
                 direct_r.at[k], dev)
        )
    for k in range(side - 1, 0, -1):
        direct_copies[k].start()

    to_core(levels, 2)

    far_copy.wait_recv()
    pack(half * side, side // 4, lambda: far[...], relay_out)
    relay_copies = [
        send(relay_out.at[inner(j)], relay_in.at[j], relay_s.at[j], relay_r.at[j],
             half * side + inner(j))
        for j in range(side)
    ]
    for j in range(side - 1, 0, -1):
        relay_copies[j].start()

    lax.fori_loop(0, levels, keep, 0)

    level_sel = [sel[back(0, k // 2, k % 2)] for k in range(LEVEL)]
    zeros = jnp.zeros((CAP, rows), F32)
    for pos in range(2):
        pieces = []
        for s in level_sel:
            pieces += [s, zeros] if pos == 0 else [zeros, s]
        place[pos] = jnp.concatenate(pieces, axis=0).T.astype(BF16)

    a_copy.wait()

    def down_map(x, at):
        n = x.shape[1]
        dims = (((1,), (1,)), ((), ()))
        t0 = lax.dot_general(
            x, a[:, pl.ds(pl.multiple_of(at, 128), n)], dims, preferred_element_type=F32
        )
        t1 = lax.dot_general(
            x, a[:, pl.ds(pl.multiple_of(at + n, 128), n)], dims, preferred_element_type=F32
        )
        return t0[:CAP] + t1[CAP:]

    low = down_map(near_out[inner(0)], me * depth)

    def direct_map(x, src, pair):
        dims = (((1,), (1,)), ((), ()))
        n = x.shape[1]
        t0 = lax.dot_general(
            x, a[:, pl.ds(pl.multiple_of(src * depth + relayed, 128), n)], dims,
            preferred_element_type=F32,
        )
        t1 = lax.dot_general(
            x, a[:, pl.ds(pl.multiple_of(pair * depth + relayed, 128), n)], dims,
            preferred_element_type=F32,
        )
        return t0[:CAP] + t1[CAP:]

    low += direct_map(direct_out[z * 2 + c], me, device(0, 1, 0))
    low += down_map(relay_out[inner(0)], ((1 - half) * side + inner(0)) * depth)
    for j in range(1, side):
        near_copies[j].wait_recv()
        low += down_map(near_in[j], (half * side + inner(j)) * depth)
    for k in range(1, side):
        direct_copies[k].wait_recv()
        low += direct_map(direct_in[k], back(k // 2, 0, k % 2), back(k // 2, 1, k % 2))
    for j in range(1, side):
        relay_copies[j].wait_recv()
        low += down_map(relay_in[j], ((1 - half) * side + inner(j)) * depth)
    low = low.astype(BF16)

    u_copy.wait()
    steps = [(2, 3), (1, 0)]
    lora_copies = {}
    for piece, dzs in enumerate(steps):
        for k in (3, 2, 1, 0):
            dy, dc = k // 2, k % 2
            value = jnp.concatenate(
                [mm(low, u[:, feature((z + dz) % levels, dy, dc)]) for dz in dzs], axis=0
            ).astype(BF16)
            i = piece * LEVEL + k
            if k == 0:
                lora_in[i] = value
            else:
                lora_out[i] = value
                lora_copies[i] = send(
                    lora_out.at[i], lora_in.at[i], lora_s.at[i], lora_r.at[i], device(0, dy, dc)
                )
                lora_copies[i].start()

    z_copies = {}
    for piece, dzs in enumerate(steps):
        for k in (1, 2, 3):
            lora_copies[piece * LEVEL + k].wait_recv()
        terms = lora_in[piece * LEVEL : (piece + 1) * LEVEL].reshape(LEVEL * 2 * CAP, width)
        for pos, dz in enumerate(dzs):
            zz = (z + dz) % levels
            y_copy(zz).wait_recv()
            t = total[zz] + y_in[zz].astype(F32) + mm(place[pos], terms)
            if dz == 0:
                result = t
            else:
                z_out[dz] = t.astype(BF16)
                z_copies[dz] = send(
                    z_out.at[dz], z_in.at[dz], z_s.at[dz], z_r.at[dz], device(dz, 0, 0)
                )
                z_copies[dz].start()
    for dz in range(1, levels):
        z_copies[dz].wait_recv()
        result = result + z_in[dz].astype(F32)
    out[...] = result.astype(out.dtype)

    far_copy.wait_send()
    for j in range(1, side):
        near_copies[j].wait_send()
        relay_copies[j].wait_send()
    aside_copy.wait_send()
    for k in range(1, side):
        direct_copies[k].wait_send()
    for i in range(2 * levels):
        core_copy(i).wait_send()
    for i in range(levels):
        y_copy(i).wait_send()
    for i in lora_copies:
        lora_copies[i].wait_send()
    for dz in range(1, levels):
        z_copies[dz].wait_send()


def fused(hidden, down_weight, adapter_down, adapter_up, ids, holder):
    parts = lax.axis_size("tp")
    levels = parts // LEVEL
    rows, depth = hidden.shape
    features = down_weight.shape[1]
    width = features // parts
    relayed = depth // 256 * 4 // 7 * 256
    direct = depth - relayed
    side = parts // 2
    vmem = pl.BlockSpec(memory_space=pltpu.VMEM)
    anywhere = pl.BlockSpec(memory_space=pl.ANY)
    dma = pltpu.SemaphoreType.DMA
    return pl.pallas_call(
        functools.partial(kernel, levels),
        out_shape=jax.ShapeDtypeStruct((rows, width), BF16),
        in_specs=[vmem, vmem, vmem, anywhere, anywhere, anywhere],
        out_specs=vmem,
        scratch_shapes=[
            pltpu.VMEM((parts, depth, width), BF16),
            pltpu.VMEM(adapter_down.shape, BF16),
            pltpu.VMEM(adapter_up.shape, BF16),
            pltpu.VMEM((parts, CAP, rows), F32),
            pltpu.VMEM((2, rows, LEVEL * 2 * CAP), BF16),
            pltpu.VMEM((rows, relayed), BF16),
            pltpu.VMEM((rows, direct), BF16),
            pltpu.VMEM((side, 2 * CAP, relayed // 2), BF16),
            pltpu.VMEM((side, 2 * CAP, relayed // 2), BF16),
            pltpu.VMEM((side, 2 * CAP, relayed // 2), BF16),
            pltpu.VMEM((side, 2 * CAP, relayed // 2), BF16),
            pltpu.VMEM((side, 2 * CAP, direct), BF16),
            pltpu.VMEM((side, 2 * CAP, direct), BF16),
            pltpu.VMEM((2 * levels, rows, width), F32),
            pltpu.VMEM((2 * levels, rows, width), F32),
            pltpu.VMEM((levels, rows, width), BF16),
            pltpu.VMEM((levels, rows, width), BF16),
            pltpu.VMEM((levels, rows, width), F32),
            pltpu.VMEM((2 * LEVEL, 2 * CAP, width), BF16),
            pltpu.VMEM((2 * LEVEL, 2 * CAP, width), BF16),
            pltpu.VMEM((levels, rows, width), BF16),
            pltpu.VMEM((levels, rows, width), BF16),
            dma((parts,)), dma, dma,
            dma, dma,
            dma, dma,
            dma((side,)), dma((side,)),
            dma((side,)), dma((side,)),
            dma((side,)), dma((side,)),
            dma((2 * levels,)), dma((2 * levels,)),
            dma((levels,)), dma((levels,)),
            dma((2 * LEVEL,)), dma((2 * LEVEL,)),
            dma((levels,)), dma((levels,)),
        ],
        compiler_params=pltpu.CompilerParams(
            collective_id=0, has_side_effects=True, vmem_limit_bytes=60 * 1024 * 1024
        ),
        cost_estimate=pl.CostEstimate(
            flops=2 * rows * depth * features,
            bytes_accessed=2 * depth * features,
            transcendentals=0,
        ),
    )(hidden, ids.reshape(1, rows), holder.reshape(1, parts), down_weight, adapter_down, adapter_up)


def general(
    hidden, down_weight, adapter_down_weight, adapter_up_weight, row_adapter_ids, adapter_holder
):
    parts = lax.axis_size("tp")
    rows = hidden.shape[0]
    holder_device = adapter_holder[row_adapter_ids]
    owners = jnp.arange(parts, dtype=jnp.int32)
    onehot = (holder_device[:, None] == owners[None, :]).astype(jnp.int32)
    within = jnp.sum(jnp.cumsum(onehot, axis=0) * onehot, axis=1) - 1
    row_ids = jnp.arange(rows, dtype=jnp.int32)
    table = jnp.full((parts, CAP), rows, jnp.int32).at[holder_device, within].set(row_ids)
    outgoing = jnp.take(hidden, table, axis=0, mode="fill", fill_value=0)
    reduced_state = jnp.einsum(
        "sf,rf->sr",
        lax.all_to_all(outgoing, "tp", split_axis=0, concat_axis=2, tiled=True)[0],
        adapter_down_weight[0],
        preferred_element_type=F32,
    ).astype(BF16)
    mine = (holder_device == lax.axis_index("tp"))[:, None]
    low = jnp.where(mine, jnp.take(reduced_state, within, axis=0, mode="clip"), 0)
    partial_sum = mm(hidden, down_weight) + mm(low, adapter_up_weight[0])
    return lax.psum_scatter(partial_sum, "tp", scatter_dimension=1, tiled=True).astype(BF16)


def local(
    hidden, down_weight, adapter_down_weight, adapter_up_weight, row_adapter_ids, adapter_holder
):
    parts = lax.axis_size("tp")
    tiled = (
        parts == 4 * LEVEL
        and hidden.shape[1] % 256 == 0
        and down_weight.shape[1] % (128 * parts) == 0
        and hidden.shape[0] == 128
        and hidden.shape[1] * down_weight.shape[1] <= 2**24
        and adapter_holder.shape[0] == parts
    )
    if tiled:
        return fused(
            hidden, down_weight, adapter_down_weight[0], adapter_up_weight[0],
            row_adapter_ids, adapter_holder,
        )
    return general(
        hidden, down_weight, adapter_down_weight, adapter_up_weight, row_adapter_ids, adapter_holder
    )


def solution(mesh):
    return jax.shard_map(
        local,
        mesh=mesh,
        in_specs=(
            P("groups", "tp"),
            P("tp", None),
            P("tp", None, None),
            P("tp", None, None),
            P("groups"),
            P(),
        ),
        out_specs=P("groups", "tp"),
        check_vma=False,
    )
```
